32 devices in a mesh: groups: 2 (over y), seq: 8 (over z, x), head: 2 (over core).
Axes of the slice: x: 2, y: 2, z: 4, core: 2. Of those that a mesh axis runs over, the one named last changes fastest.
Arguments:
- queries: bfloat16 [256, 3072], P(('groups', 'seq'), 'head'), parts along dimension 0, may hold values from -300 to 300, as said below
- latent: bfloat16 [512, 256], P(None, ('groups', 'seq')), parts along dimension 1, may hold values from -6 to 6
- key_basis: bfloat16 [512, 3072], P(None, 'head'), may hold values from -0.25 to 0.25
- value_basis: bfloat16 [512, 3072], P(None, 'head'), may hold values from -0.25 to 0.25
- out_weight: bfloat16 [3072, 3072], P('seq', 'head'), may hold values from -0.625 to 0.625
Outputs:
- attended: bfloat16 [256, 3072], P(('groups', 'seq'), 'head'), parts along dimension 0
The draws below stay inside these ranges and needn't reach their ends.
There are 2 independent parts, one for each index of `groups`. The reference program is written for one: setup_inputs(seed, part) draws one part's arguments, and reference() takes and returns one part's arrays. A program takes and returns all parts, laid end to end along the dimension named above; an argument that names none is the same for every part. Nothing has to cross between parts.
Inputs may be any that keep to these rules, and one draw needn't show every extreme that they name: `queries`: real-valued entries.
All inputs are finite; a program needn't handle non-finite values.
Results may differ from the reference program's by a relative error of at most 0.0099.
Values may be sent and summed in bfloat16 or wider, within the bound.
No kernel may reach another device: no remote copies, remote signals or barrier semaphores. Data moves between devices by JAX's collectives and lax.ppermute only.
A program may use at most 64 MiB of HBM per device.

```python
import math
import jax
import jax.numpy as jnp
from jax import lax

D = 3072
HEADS = 24
HEAD_DIM = 128
RANK = 512
TOKENS = 128


def draw_queries(key, part):
    first = jax.random.fold_in(jax.random.fold_in(key, 11), 0)
    values = jax.random.normal(first, (TOKENS, HEADS * HEAD_DIM), jnp.float32) * 1.4
    return jnp.clip(values, -300.0, 300.0).astype(jnp.bfloat16)


def levels(stream_key, extent, shards, least, top_value):
    def one(position, parts):
        draws = jax.random.uniform(jax.random.fold_in(jax.random.fold_in(stream_key, 6), position), (parts,), jnp.float32, least / len(shards), top_value / len(shards))
        return jnp.repeat(jnp.exp(draws), extent[position] // parts).reshape((-1,) + (1,) * (len(extent) - position - 1))

    loudness = one(*shards[0])
    for cut in shards[1:]:
        loudness = loudness * one(*cut)
    return loudness


def gaussian(rng, extent, scale, reach, cuts=(), kind=jnp.bfloat16):
    level = levels(rng, extent, cuts, -0.22, 0.18) if cuts else 1.0
    drawn = jax.random.normal(rng, extent, jnp.float32) * scale * level
    return jnp.minimum(jnp.maximum(drawn, -reach), reach).astype(kind)


def setup_inputs(seed: int = 0, part: int = 0) -> dict:
    splits = jax.random.split(jax.random.key(seed), 6)
    part_splits = jax.random.split(jax.random.fold_in(splits[5], part), 6)
    queries = draw_queries(jax.random.fold_in(jax.random.fold_in(splits[5], part), 71), part)
    latent = gaussian(part_splits[1], (RANK, TOKENS), 1.0, 6.0, ((1, 8),))
    key_basis = gaussian(splits[2], (RANK, HEADS * HEAD_DIM), RANK ** -0.5, 0.25, ((1, 2),))
    value_basis = gaussian(splits[3], (RANK, HEADS * HEAD_DIM), RANK ** -0.5, 0.25, ((1, 2),))
    out_weight = gaussian(splits[4], (D, HEADS * HEAD_DIM), (HEADS * HEAD_DIM // 32) ** -0.5, 0.625, ((0, 8), (1, 2)))
    return {"queries": queries, "latent": latent, "key_basis": key_basis, "value_basis": value_basis, "out_weight": out_weight}


def attend(queries, latent, key_basis, value_basis):
    tok_rows = queries.shape[0]
    head_count = key_basis.shape[1] // HEAD_DIM
    rank_count = key_basis.shape[0]
    score_scale = 1.0 / math.sqrt(HEAD_DIM)
    query_heads = queries.reshape(tok_rows, head_count, HEAD_DIM).transpose(1, 0, 2)
    key_maps = key_basis.reshape(rank_count, head_count, HEAD_DIM).transpose(1, 0, 2)
    value_maps = value_basis.reshape(rank_count, head_count, HEAD_DIM).transpose(1, 0, 2)

    def one_head(operands):
        query_one, key_map, value_map = operands
        key_rows = lax.dot_general(latent, key_map, (((0,), (0,)), ((), ())), preferred_element_type=jnp.float32).astype(jnp.bfloat16)
        value_rows = lax.dot_general(latent, value_map, (((0,), (0,)), ((), ())), preferred_element_type=jnp.float32).astype(jnp.bfloat16)
        scores = lax.dot_general(query_one, key_rows, (((1,), (1,)), ((), ())), preferred_element_type=jnp.float32) * score_scale
        row_max = lax.optimization_barrier(jnp.max(scores, axis=1, keepdims=True))
        weights = jnp.exp(scores - row_max)
        row_total = lax.optimization_barrier(jnp.sum(weights, axis=1, keepdims=True))
        head_mixed = jnp.dot(weights.astype(jnp.bfloat16), value_rows, preferred_element_type=jnp.float32) / row_total
        return head_mixed.astype(jnp.bfloat16)
    mixed = lax.map(one_head, (query_heads, key_maps, value_maps))
    return mixed.transpose(1, 0, 2).reshape(tok_rows, head_count * HEAD_DIM)

def reference(queries, latent, key_basis, value_basis, out_weight):
    mixed = attend(queries, latent, key_basis, value_basis)
    attended = lax.dot_general(mixed, out_weight, (((1,), (1,)), ((), ())), preferred_element_type=jnp.float32)
    return attended.astype(jnp.bfloat16)
```

```python
import functools
import math

import jax
import jax.numpy as jnp
from jax import lax
from jax.experimental import pallas as pl
from jax.experimental.pallas import tpu as pltpu
from jax.sharding import PartitionSpec as P

HEAD_DIM = 128
MOST_DIRECT = 16
NT = (((1,), (1,)), ((), ()))


def mix_kernel(count, *refs):
    blocks = refs[:count]
    key_basis, value_basis, out_weight, keep, send, mixed, partial_sum = refs[count:]
    width = key_basis.shape[1]
    queries = jnp.concatenate([b[:, :width] for b in blocks], axis=0)
    latent = jnp.concatenate([b[:, width:] for b in blocks], axis=0)
    scale = 1.0 / math.sqrt(HEAD_DIM)
    for first in range(0, width, HEAD_DIM):
        cols = slice(first, first + HEAD_DIM)
        keys = jnp.dot(latent, key_basis[:, cols], preferred_element_type=jnp.float32)
        values = jnp.dot(latent, value_basis[:, cols], preferred_element_type=jnp.float32)
        scores = (
            lax.dot_general(
                queries[:, cols], keys.astype(jnp.bfloat16), NT, preferred_element_type=jnp.float32
            )
            * scale
        )
        weights = jnp.exp(scores - jnp.max(scores, axis=1, keepdims=True))
        totals = jnp.sum(weights, axis=1, keepdims=True)
        head = jnp.dot(
            weights.astype(jnp.bfloat16),
            values.astype(jnp.bfloat16),
            preferred_element_type=jnp.float32,
        )
        mixed[:, cols] = (head / totals).astype(jnp.bfloat16)
    partial_sum[...] = lax.dot_general(
        mixed[...], out_weight[...], NT, preferred_element_type=jnp.float32
    )
    rows = keep.shape[0]
    core = lax.axis_index("head")
    keep[...] = partial_sum[pl.ds(pl.multiple_of(core * rows, rows), rows), :]
    send[...] = partial_sum[pl.ds(pl.multiple_of((1 - core) * rows, rows), rows), :]


def mix(blocks, key_basis, value_basis, out_weight):
    rows = sum(b.shape[0] for b in blocks)
    width, features = key_basis.shape[1], out_weight.shape[0]
    half = jax.ShapeDtypeStruct((rows // 2, features), jnp.float32)
    vmem = pl.BlockSpec(memory_space=pltpu.VMEM)
    rank = key_basis.shape[0]
    return pl.pallas_call(
        functools.partial(mix_kernel, len(blocks)),
        out_shape=(half, half),
        in_specs=[vmem] * (len(blocks) + 3),
        out_specs=(vmem, vmem),
        scratch_shapes=[
            pltpu.VMEM((rows, width), jnp.bfloat16),
            pltpu.VMEM((rows, features), jnp.float32),
        ],
        cost_estimate=pl.CostEstimate(
            flops=2 * rows * width * (2 * rank + 2 * rows + features),
            bytes_accessed=2 * width * (2 * rank + features),
            transcendentals=rows * rows * (width // HEAD_DIM),
        ),
        compiler_params=pltpu.CompilerParams(vmem_limit_bytes=32 * 1024 * 1024),
        name="mix",
    )(*blocks, key_basis, value_basis, out_weight)


def place_kernel(half, *refs):
    parts, out = refs[:-1], refs[-1]
    features = parts[0].shape[1]
    mine = lax.rem(lax.axis_index("seq"), half)
    for step, part in enumerate(parts):
        column = jnp.bitwise_xor(mine, step) * features
        out[:, pl.ds(pl.multiple_of(column, features), features)] = part[...]


def place(parts, half):
    rows, features = parts[0].shape
    vmem = pl.BlockSpec(memory_space=pltpu.VMEM)
    return pl.pallas_call(
        functools.partial(place_kernel, half),
        out_shape=jax.ShapeDtypeStruct((rows, features * half), parts[0].dtype),
        in_specs=[vmem] * len(parts),
        out_specs=vmem,
        name="place",
    )(*parts)


def direct(count, queries, latent, key_basis, value_basis, out_weight):
    rows, half = queries.shape[0], count // 2
    own = jnp.concatenate([queries, latent.T], axis=1)
    blocks = {0: own}
    for flip in reversed(range(1, count)):
        blocks[flip] = lax.ppermute(own, "seq", [(i, i ^ flip) for i in range(count)])
    keep, send = mix([blocks[k] for k in range(count)], key_basis, value_basis, out_weight)
    other = lax.ppermute(send, "head", [(0, 1), (1, 0)])
    total = (keep + other).astype(jnp.bfloat16)
    parts = [None] * half
    for step in reversed(range(half)):
        pairs = [
            (2 * s + h, 2 * (s ^ (step + h * half)) + s // half)
            for s in range(count)
            for h in range(2)
        ]
        parts[step] = lax.ppermute(
            total[step * rows : (step + 1) * rows], ("seq", "head"), pairs
        )
    return place(parts, half)


def attend(queries, latent, key_basis, value_basis):
    tok_rows = queries.shape[0]
    head_count = key_basis.shape[1] // HEAD_DIM
    rank_count = key_basis.shape[0]
    score_scale = 1.0 / math.sqrt(HEAD_DIM)
    query_heads = queries.reshape(tok_rows, head_count, HEAD_DIM).transpose(1, 0, 2)
    key_maps = key_basis.reshape(rank_count, head_count, HEAD_DIM).transpose(1, 0, 2)
    value_maps = value_basis.reshape(rank_count, head_count, HEAD_DIM).transpose(1, 0, 2)

    def one_head(operands):
        query_one, key_map, value_map = operands
        key_rows = lax.dot_general(
            latent, key_map, (((0,), (0,)), ((), ())), preferred_element_type=jnp.float32
        ).astype(jnp.bfloat16)
        value_rows = lax.dot_general(
            latent, value_map, (((0,), (0,)), ((), ())), preferred_element_type=jnp.float32
        ).astype(jnp.bfloat16)
        scores = (
            lax.dot_general(query_one, key_rows, NT, preferred_element_type=jnp.float32)
            * score_scale
        )
        row_max = jnp.max(scores, axis=1, keepdims=True)
        weights = jnp.exp(scores - row_max)
        row_total = jnp.sum(weights, axis=1, keepdims=True)
        head_mixed = (
            jnp.dot(weights.astype(jnp.bfloat16), value_rows, preferred_element_type=jnp.float32)
            / row_total
        )
        return head_mixed.astype(jnp.bfloat16)

    mixed = lax.map(one_head, (query_heads, key_maps, value_maps))
    return mixed.transpose(1, 0, 2).reshape(tok_rows, head_count * HEAD_DIM)


def gathered(queries, latent, key_basis, value_basis, out_weight):
    latent = lax.all_gather(latent, "seq", axis=1, tiled=True)
    mixed = attend(queries, latent, key_basis, value_basis)
    weight = lax.all_gather(out_weight, "seq", axis=0, tiled=True)
    partial_value = lax.dot_general(mixed, weight, NT, preferred_element_type=jnp.float32)
    return lax.psum_scatter(partial_value, "head", scatter_dimension=1, tiled=True).astype(
        jnp.bfloat16
    )


def solution(mesh):
    placed = (
        P(("groups", "seq"), "head"),
        P(None, ("groups", "seq")),
        P(None, "head"),
        P(None, "head"),
        P("seq", "head"),
    )
    count = mesh.shape["seq"]
    pairwise = 2 <= count <= MOST_DIRECT and count & (count - 1) == 0 and mesh.shape["head"] == 2
    shards = functools.partial(direct, count) if pairwise else gathered
    return jax.shard_map(
        shards, mesh=mesh, in_specs=placed, out_specs=P(("groups", "seq"), "head"), check_vma=False
    )
```

```python
import functools
import math

import jax
import jax.numpy as jnp
from jax import lax
from jax.experimental import pallas as pl
from jax.experimental.pallas import tpu as pltpu
from jax.sharding import PartitionSpec as P

HEAD_DIM = 128
MOST_DIRECT = 16
NT = (((1,), (1,)), ((), ()))


def hold_kernel(*refs):
    count = (len(refs) - 1) // 2
    copies = [
        pltpu.make_async_copy(source, kept, refs[-1].at[i])
        for i, (source, kept) in enumerate(zip(refs[:count], refs[count:-1]))
    ]
    for copy in copies:
        copy.start()
    for copy in copies:
        copy.wait()


def hold(*weights):
    vmem = pl.BlockSpec(memory_space=pltpu.VMEM)
    return pl.pallas_call(
        hold_kernel,
        out_shape=[jax.ShapeDtypeStruct(w.shape, w.dtype) for w in weights],
        in_specs=[pl.BlockSpec(memory_space=pltpu.HBM)] * len(weights),
        out_specs=[vmem] * len(weights),
        scratch_shapes=[pltpu.SemaphoreType.DMA((len(weights),))],
        cost_estimate=pl.CostEstimate(
            flops=0, bytes_accessed=sum(4 * w.size for w in weights), transcendentals=0
        ),
        compiler_params=pltpu.CompilerParams(vmem_limit_bytes=1024 * 1024),
        name="hold",
    )(*(pltpu.with_memory_space_constraint(w, pltpu.HBM) for w in weights))


def mix_kernel(count, half, *refs):
    blocks = refs[:count]
    key_basis, value_basis, out_weight, keep, send, partial_sum = refs[count:]
    width = key_basis.shape[1]
    queries = jnp.concatenate([b[:, :width] for b in blocks], axis=0)
    latent = jnp.concatenate([b[:, width:] for b in blocks], axis=0)
    scale = 1.0 / math.sqrt(HEAD_DIM)
    heads = [slice(first, first + HEAD_DIM) for first in range(0, width, HEAD_DIM)]
    keys = jnp.dot(latent, key_basis[...], preferred_element_type=jnp.float32).astype(jnp.bfloat16)
    values = jnp.dot(latent, value_basis[...], preferred_element_type=jnp.float32).astype(
        jnp.bfloat16
    )
    scores = [
        lax.dot_general(queries[:, c], keys[:, c], NT, preferred_element_type=jnp.float32) * scale
        for c in heads
    ]
    weights = [jnp.exp(s - jnp.max(s, axis=1, keepdims=True)) for s in scores]
    totals = [jnp.sum(w, axis=1, keepdims=True) for w in weights]
    sums = [
        jnp.dot(w.astype(jnp.bfloat16), values[:, c], preferred_element_type=jnp.float32)
        for w, c in zip(weights, heads)
    ]
    mixed = jnp.concatenate([(s / t).astype(jnp.bfloat16) for s, t in zip(sums, totals)], axis=1)
    partial_sum[...] = lax.dot_general(
        mixed, out_weight[...], NT, preferred_element_type=jnp.float32
    )
    rows = keep.shape[0]
    far = own_half(half)
    keep[...] = partial_sum[pl.ds(pl.multiple_of(far * rows, rows), rows), :]
    send[...] = partial_sum[pl.ds(pl.multiple_of((1 - far) * rows, rows), rows), :]


def own_half(half):
    taker = lax.axis_index("seq") // half
    return 1 - jnp.bitwise_xor(taker, lax.axis_index("head"))


def mix(half, blocks, key_basis, value_basis, out_weight):
    rows = sum(b.shape[0] for b in blocks)
    width, features = key_basis.shape[1], out_weight.shape[0]
    rank = key_basis.shape[0]
    vmem = pl.BlockSpec(memory_space=pltpu.VMEM)
    return pl.pallas_call(
        functools.partial(mix_kernel, len(blocks), half),
        out_shape=[jax.ShapeDtypeStruct((rows // 2, features), jnp.float32)] * 2,
        in_specs=[vmem] * (len(blocks) + 3),
        out_specs=[vmem] * 2,
        scratch_shapes=[pltpu.VMEM((rows, features), jnp.float32)],
        cost_estimate=pl.CostEstimate(
            flops=2 * rows * width * (2 * rank + 2 * rows + features),
            bytes_accessed=2 * width * (2 * rank + features),
            transcendentals=rows * rows * (width // HEAD_DIM),
        ),
        compiler_params=pltpu.CompilerParams(vmem_limit_bytes=16 * 1024 * 1024),
        name="mix",
    )(*blocks, key_basis, value_basis, out_weight)


def place_kernel(half, *refs):
    parts, out = refs[:-1], refs[-1]
    features = parts[0].shape[1]
    mine = lax.rem(lax.axis_index("seq"), half)
    for step, part in enumerate(parts):
        column = jnp.bitwise_xor(mine, step) * features
        out[:, pl.ds(pl.multiple_of(column, features), features)] = part[...]


def place(parts, half):
    rows, features = parts[0].shape
    vmem = pl.BlockSpec(memory_space=pltpu.VMEM)
    return pl.pallas_call(
        functools.partial(place_kernel, half),
        out_shape=jax.ShapeDtypeStruct((rows, features * half), parts[0].dtype),
        in_specs=[vmem] * len(parts),
        out_specs=vmem,
        compiler_params=pltpu.CompilerParams(vmem_limit_bytes=1024 * 1024),
        name="place",
    )(*parts)


def back(count, step):
    half = count // 2
    pairs = []
    for s in range(count):
        taker = s // half
        pairs.append((2 * s + taker, 2 * (s ^ (step + half)) + taker))
        pairs.append((2 * s + 1 - taker, 2 * (s ^ step) + taker))
    return pairs


def direct(count, queries, latent, key_basis, value_basis, out_weight):
    rows, half = queries.shape[0], count // 2
    own = jnp.concatenate([queries, latent.T], axis=1)
    blocks = {0: own}
    for flip in flips(count):
        blocks[flip] = lax.ppermute(own, "seq", [(i, i ^ flip) for i in range(count)])
    weights = hold(key_basis, value_basis, out_weight)
    keep, send = mix(half, [blocks[k] for k in range(count)], *weights)
    other = lax.ppermute(send, "head", [(0, 1), (1, 0)])
    total = (keep + other).astype(jnp.bfloat16)
    parts = [None] * half
    for step in reversed(range(half)):
        parts[step] = lax.ppermute(
            total[step * rows : (step + 1) * rows], ("seq", "head"), back(count, step)
        )
    return place(parts, half)


def flips(count):
    return (4, 5, 7, 6, 3, 1, 2) if count == 8 else tuple(reversed(range(1, count)))


def attend(queries, latent, key_basis, value_basis):
    tok_rows = queries.shape[0]
    head_count = key_basis.shape[1] // HEAD_DIM
    rank_count = key_basis.shape[0]
    score_scale = 1.0 / math.sqrt(HEAD_DIM)
    query_heads = queries.reshape(tok_rows, head_count, HEAD_DIM).transpose(1, 0, 2)
    key_maps = key_basis.reshape(rank_count, head_count, HEAD_DIM).transpose(1, 0, 2)
    value_maps = value_basis.reshape(rank_count, head_count, HEAD_DIM).transpose(1, 0, 2)

    def one_head(operands):
        query_one, key_map, value_map = operands
        key_rows = lax.dot_general(
            latent, key_map, (((0,), (0,)), ((), ())), preferred_element_type=jnp.float32
        ).astype(jnp.bfloat16)
        value_rows = lax.dot_general(
            latent, value_map, (((0,), (0,)), ((), ())), preferred_element_type=jnp.float32
        ).astype(jnp.bfloat16)
        scores = (
            lax.dot_general(query_one, key_rows, NT, preferred_element_type=jnp.float32)
            * score_scale
        )
        row_max = jnp.max(scores, axis=1, keepdims=True)
        weights = jnp.exp(scores - row_max)
        row_total = jnp.sum(weights, axis=1, keepdims=True)
        head_mixed = (
            jnp.dot(weights.astype(jnp.bfloat16), value_rows, preferred_element_type=jnp.float32)
            / row_total
        )
        return head_mixed.astype(jnp.bfloat16)

    mixed = lax.map(one_head, (query_heads, key_maps, value_maps))
    return mixed.transpose(1, 0, 2).reshape(tok_rows, head_count * HEAD_DIM)


def gathered(queries, latent, key_basis, value_basis, out_weight):
    latent = lax.all_gather(latent, "seq", axis=1, tiled=True)
    mixed = attend(queries, latent, key_basis, value_basis)
    weight = lax.all_gather(out_weight, "seq", axis=0, tiled=True)
    partial_value = lax.dot_general(mixed, weight, NT, preferred_element_type=jnp.float32)
    return lax.psum_scatter(partial_value, "head", scatter_dimension=1, tiled=True).astype(
        jnp.bfloat16
    )


def solution(mesh):
    placed = (
        P(("groups", "seq"), "head"),
        P(None, ("groups", "seq")),
        P(None, "head"),
        P(None, "head"),
        P("seq", "head"),
    )
    count = mesh.shape["seq"]
    pairwise = 2 <= count <= MOST_DIRECT and count & (count - 1) == 0 and mesh.shape["head"] == 2
    shards = functools.partial(direct, count) if pairwise else gathered
    return jax.shard_map(
        shards, mesh=mesh, in_specs=placed, out_specs=P(("groups", "seq"), "head"), check_vma=False
    )
```

```python
import functools
import math

import jax
import jax.numpy as jnp
from jax import lax
from jax.experimental import pallas as pl
from jax.experimental.pallas import tpu as pltpu
from jax.sharding import PartitionSpec as P

HEAD_DIM = 128
MOST_DIRECT = 16
NT = (((1,), (1,)), ((), ()))


def hold_kernel(*refs):
    count = (len(refs) - 1) // 2
    copies = [
        pltpu.make_async_copy(source, kept, refs[-1].at[i])
        for i, (source, kept) in enumerate(zip(refs[:count], refs[count:-1]))
    ]
    for copy in copies:
        copy.start()
    for copy in copies:
        copy.wait()


def hold(*weights):
    vmem = pl.BlockSpec(memory_space=pltpu.VMEM)
    return pl.pallas_call(
        hold_kernel,
        out_shape=[jax.ShapeDtypeStruct(w.shape, w.dtype) for w in weights],
        in_specs=[pl.BlockSpec(memory_space=pltpu.HBM)] * len(weights),
        out_specs=[vmem] * len(weights),
        scratch_shapes=[pltpu.SemaphoreType.DMA((len(weights),))],
        cost_estimate=pl.CostEstimate(
            flops=0, bytes_accessed=sum(4 * w.size for w in weights), transcendentals=0
        ),
        compiler_params=pltpu.CompilerParams(vmem_limit_bytes=1024 * 1024),
        name="hold",
    )(*(pltpu.with_memory_space_constraint(w, pltpu.HBM) for w in weights))


def mix_kernel(plan, *refs):
    blocks = [refs[plan.order.index(flip)] for flip in range(plan.count)]
    key_basis, value_basis, out_weight, keep, send, partial_sum = refs[plan.count :]
    rows = blocks[0].shape[0]
    width = key_basis.shape[1]
    queries = jnp.concatenate([b[:, :width] for b in blocks], axis=0)
    latent = jnp.concatenate([b[:, width:] for b in blocks], axis=0)
    scale = 1.0 / math.sqrt(HEAD_DIM)
    heads = [slice(first, first + HEAD_DIM) for first in range(0, width, HEAD_DIM)]
    keys = jnp.dot(latent, key_basis[...], preferred_element_type=jnp.float32).astype(jnp.bfloat16)
    values = jnp.dot(latent, value_basis[...], preferred_element_type=jnp.float32).astype(
        jnp.bfloat16
    )
    scores = [
        lax.dot_general(queries[:, c], keys[:, c], NT, preferred_element_type=jnp.float32) * scale
        for c in heads
    ]
    weights = [jnp.exp(s - jnp.max(s, axis=1, keepdims=True)) for s in scores]
    totals = [jnp.sum(w, axis=1, keepdims=True) for w in weights]
    sums = [
        jnp.dot(w.astype(jnp.bfloat16), values[:, c], preferred_element_type=jnp.float32)
        for w, c in zip(weights, heads)
    ]
    mixed = jnp.concatenate([(s / t).astype(jnp.bfloat16) for s, t in zip(sums, totals)], axis=1)
    partial_sum[...] = lax.dot_general(
        mixed, out_weight[...], NT, preferred_element_type=jnp.float32
    )
    taker = lax.axis_index("head") == lax.axis_index("seq") // plan.half
    for step, flips in enumerate(plan.turns):
        first, second = (partial_sum[flip * rows : (flip + 1) * rows, :] for flip in flips)
        part = slice(step * rows, (step + 1) * rows)
        keep[part, :] = jnp.where(taker, first, second)
        send[part, :] = jnp.where(taker, second, first)


def mix(plan, blocks, key_basis, value_basis, out_weight):
    rows = blocks[0].shape[0] * plan.count
    rank, width = key_basis.shape
    features = out_weight.shape[0]
    vmem = pl.BlockSpec(memory_space=pltpu.VMEM)
    return pl.pallas_call(
        functools.partial(mix_kernel, plan),
        out_shape=[jax.ShapeDtypeStruct((rows // 2, features), jnp.float32)] * 2,
        in_specs=[vmem] * (plan.count + 3),
        out_specs=[vmem] * 2,
        scratch_shapes=[pltpu.VMEM((rows, features), jnp.float32)],
        cost_estimate=pl.CostEstimate(
            flops=2 * rows * width * (2 * rank + 2 * rows + features),
            bytes_accessed=2 * width * (2 * rank + features),
            transcendentals=rows * rows * (width // HEAD_DIM),
        ),
        compiler_params=pltpu.CompilerParams(vmem_limit_bytes=16 * 1024 * 1024),
        name="mix",
    )(*(blocks[flip] for flip in plan.order), key_basis, value_basis, out_weight)


def place_kernel(plan, *refs):
    parts, out = refs[:-1], refs[-1]
    features = parts[0].shape[1]
    seq = lax.axis_index("seq")
    near = seq // plan.half == lax.axis_index("head")
    for step, part in zip(plan.landed, parts):
        low, high = sorted(plan.turns[step])
        flip = jnp.where(near, low, high - plan.half)
        column = jnp.bitwise_xor(lax.rem(seq, plan.half), flip) * features
        out[:, pl.ds(pl.multiple_of(column, features), features)] = part[...]


def place(plan, parts):
    rows, features = parts[0].shape
    vmem = pl.BlockSpec(memory_space=pltpu.VMEM)
    return pl.pallas_call(
        functools.partial(place_kernel, plan),
        out_shape=jax.ShapeDtypeStruct((rows, features * plan.half), parts[0].dtype),
        in_specs=[vmem] * len(parts),
        out_specs=vmem,
        compiler_params=pltpu.CompilerParams(vmem_limit_bytes=1024 * 1024),
        name="place",
    )(*parts)


class Plan:
    def __init__(self, count):
        self.count, self.half = count, count // 2
        if count == 8:
            self.out, self.again = (3, 2, 1), (3, 2, 1)
            self.turns = ((7, 2), (5, 3), (4, 0), (6, 1))
        else:
            self.out = self.again = tuple(reversed(range(1, self.half)))
            self.turns = tuple((i + self.half, i) for i in reversed(range(self.half)))
        sent = (self.half, *self.out, *(flip + self.half for flip in self.again))
        self.order = (0, *reversed(sent))
        self.landed = tuple(reversed(range(self.half)))

    def flip(self, flip):
        return [(i, i ^ flip) for i in range(self.count)]

    def back(self, step):
        pairs = []
        for s in range(self.count):
            taker = s // self.half
            for core, flip in zip((taker, 1 - taker), self.turns[step]):
                pairs.append((2 * s + core, 2 * (s ^ flip) + taker))
        return pairs


def direct(plan, queries, latent, key_basis, value_basis, out_weight):
    rows, half = queries.shape[0], plan.half
    own = jnp.concatenate([queries, latent.T], axis=1)
    across = lax.ppermute(own, "seq", plan.flip(half))
    blocks = {0: own, half: across}
    for flip in plan.out:
        blocks[flip] = lax.ppermute(own, "seq", plan.flip(flip))
    for flip in plan.again:
        blocks[flip + half] = lax.ppermute(across, "seq", plan.flip(flip))
    weights = hold(key_basis, value_basis, out_weight)
    keep, send = mix(plan, blocks, *weights)
    other = lax.ppermute(send, "head", [(0, 1), (1, 0)])
    total = (keep + other).astype(jnp.bfloat16)
    parts = [
        lax.ppermute(total[step * rows : (step + 1) * rows], ("seq", "head"), plan.back(step))
        for step in plan.landed
    ]
    return place(plan, parts)


def attend(queries, latent, key_basis, value_basis):
    tok_rows = queries.shape[0]
    head_count = key_basis.shape[1] // HEAD_DIM
    rank_count = key_basis.shape[0]
    score_scale = 1.0 / math.sqrt(HEAD_DIM)
    query_heads = queries.reshape(tok_rows, head_count, HEAD_DIM).transpose(1, 0, 2)
    key_maps = key_basis.reshape(rank_count, head_count, HEAD_DIM).transpose(1, 0, 2)
    value_maps = value_basis.reshape(rank_count, head_count, HEAD_DIM).transpose(1, 0, 2)

    def one_head(operands):
        query_one, key_map, value_map = operands
        key_rows = lax.dot_general(
            latent, key_map, (((0,), (0,)), ((), ())), preferred_element_type=jnp.float32
        ).astype(jnp.bfloat16)
        value_rows = lax.dot_general(
            latent, value_map, (((0,), (0,)), ((), ())), preferred_element_type=jnp.float32
        ).astype(jnp.bfloat16)
        scores = (
            lax.dot_general(query_one, key_rows, NT, preferred_element_type=jnp.float32)
            * score_scale
        )
        row_max = jnp.max(scores, axis=1, keepdims=True)
        weights = jnp.exp(scores - row_max)
        row_total = jnp.sum(weights, axis=1, keepdims=True)
        head_mixed = (
            jnp.dot(weights.astype(jnp.bfloat16), value_rows, preferred_element_type=jnp.float32)
            / row_total
        )
        return head_mixed.astype(jnp.bfloat16)

    mixed = lax.map(one_head, (query_heads, key_maps, value_maps))
    return mixed.transpose(1, 0, 2).reshape(tok_rows, head_count * HEAD_DIM)


def gathered(queries, latent, key_basis, value_basis, out_weight):
    latent = lax.all_gather(latent, "seq", axis=1, tiled=True)
    mixed = attend(queries, latent, key_basis, value_basis)
    weight = lax.all_gather(out_weight, "seq", axis=0, tiled=True)
    partial_value = lax.dot_general(mixed, weight, NT, preferred_element_type=jnp.float32)
    return lax.psum_scatter(partial_value, "head", scatter_dimension=1, tiled=True).astype(
        jnp.bfloat16
    )


def solution(mesh):
    placed = (
        P(("groups", "seq"), "head"),
        P(None, ("groups", "seq")),
        P(None, "head"),
        P(None, "head"),
        P("seq", "head"),
    )
    count = mesh.shape["seq"]
    pairwise = 4 <= count <= MOST_DIRECT and count & (count - 1) == 0 and mesh.shape["head"] == 2
    shards = functools.partial(direct, Plan(count)) if pairwise else gathered
    return jax.shard_map(
        shards, mesh=mesh, in_specs=placed, out_specs=P(("groups", "seq"), "head"), check_vma=False
    )
```

```python
import functools
import math

import jax
import jax.numpy as jnp
from jax import lax
from jax.experimental import pallas as pl
from jax.experimental.pallas import tpu as pltpu
from jax.sharding import PartitionSpec as P

HEAD_DIM = 128
MOST_DIRECT = 16
NT = (((1,), (1,)), ((), ()))


def mix_kernel(plan, own, *refs):
    received = refs[: len(plan.routes)][::-1]
    key_basis, value_basis, out_weight, keep, send, partial_sum = refs[len(plan.routes) :]
    rows = own.shape[0]
    width = key_basis.shape[1]
    queries = jnp.concatenate([b[:, :width] for b in (own, *received)], axis=0)
    latent = jnp.concatenate([b[:, width:] for b in (own, *received)], axis=0)
    scale = 1.0 / math.sqrt(HEAD_DIM)
    heads = [slice(first, first + HEAD_DIM) for first in range(0, width, HEAD_DIM)]
    keys = jnp.dot(latent, key_basis[...], preferred_element_type=jnp.float32).astype(jnp.bfloat16)
    values = jnp.dot(latent, value_basis[...], preferred_element_type=jnp.float32).astype(
        jnp.bfloat16
    )
    scores = [
        lax.dot_general(queries[:, c], keys[:, c], NT, preferred_element_type=jnp.float32) * scale
        for c in heads
    ]
    weights = [jnp.exp(s - jnp.max(s, axis=1, keepdims=True)) for s in scores]
    totals = [jnp.sum(w, axis=1, keepdims=True) for w in weights]
    sums = [
        jnp.dot(w.astype(jnp.bfloat16), values[:, c], preferred_element_type=jnp.float32)
        for w, c in zip(weights, heads)
    ]
    mixed = jnp.concatenate([(s / t).astype(jnp.bfloat16) for s, t in zip(sums, totals)], axis=1)
    partial_sum[...] = lax.dot_general(
        mixed, out_weight[...], NT, preferred_element_type=jnp.float32
    )
    taker = lax.axis_index("head") == lax.axis_index("seq") // plan.half
    for step, flips in enumerate(plan.turns):
        first, second = (
            partial_sum[at * rows : (at + 1) * rows, :] for at in map(plan.held.index, flips)
        )
        part = slice(step * rows, (step + 1) * rows)
        keep[part, :] = jnp.where(taker, first, second)
        send[part, :] = jnp.where(taker, second, first)


def mix(plan, own, received, key_basis, value_basis, out_weight):
    rows = own.shape[0] * plan.count
    rank, width = key_basis.shape
    features = out_weight.shape[0]
    vmem = pl.BlockSpec(memory_space=pltpu.VMEM)
    return pl.pallas_call(
        functools.partial(mix_kernel, plan),
        out_shape=[jax.ShapeDtypeStruct((rows // 2, features), jnp.float32)] * 2,
        in_specs=[vmem] * (len(received) + 4),
        out_specs=[vmem] * 2,
        scratch_shapes=[pltpu.VMEM((rows, features), jnp.float32)],
        cost_estimate=pl.CostEstimate(
            flops=2 * rows * width * (2 * rank + 2 * rows + features),
            bytes_accessed=2 * width * (2 * rank + features),
            transcendentals=rows * rows * (width // HEAD_DIM),
        ),
        compiler_params=pltpu.CompilerParams(vmem_limit_bytes=16 * 1024 * 1024),
        name="mix",
    )(own, *received[::-1], key_basis, value_basis, out_weight)


def place_kernel(plan, *refs):
    parts, out = refs[:-1], refs[-1]
    features = parts[0].shape[1]
    seq = lax.axis_index("seq")
    near = seq // plan.half == lax.axis_index("head")
    for step, part in zip(plan.landed, parts):
        low, high = sorted(plan.turns[step])
        flip = jnp.where(near, low, high - plan.half)
        column = jnp.bitwise_xor(lax.rem(seq, plan.half), flip) * features
        out[:, pl.ds(pl.multiple_of(column, features), features)] = part[...]


def place(plan, parts):
    rows, features = parts[0].shape
    vmem = pl.BlockSpec(memory_space=pltpu.VMEM)
    return pl.pallas_call(
        functools.partial(place_kernel, plan),
        out_shape=jax.ShapeDtypeStruct((rows, features * plan.half), parts[0].dtype),
        in_specs=[vmem] * len(parts),
        out_specs=vmem,
        compiler_params=pltpu.CompilerParams(vmem_limit_bytes=1024 * 1024),
        name="place",
    )(*parts)


def pack_kernel(block, own):
    own[...] = block[...]


def pack(block, meanwhile):
    vmem = pl.BlockSpec(memory_space=pltpu.VMEM)
    return pl.pallas_call(
        pack_kernel,
        out_shape=jax.ShapeDtypeStruct(block.shape, block.dtype),
        in_specs=[vmem],
        out_specs=vmem,
        cost_estimate=pl.CostEstimate(
            flops=4096 * meanwhile, bytes_accessed=0, transcendentals=0
        ),
        compiler_params=pltpu.CompilerParams(vmem_limit_bytes=1024 * 1024),
        name="pack",
    )(block)


class Plan:
    def __init__(self, count):
        self.count, self.half = count, count // 2
        if count == 8:
            self.routes = ((1, (0,)), (6, (0,)), (4, (0,)), (2, (0,)), (4, (1,)), (2, (1,)), (1, (6,)))
            self.turns = ((5, 3), (6, 0), (7, 2), (4, 1))
        else:
            inner = tuple(reversed(range(1, self.half)))
            self.routes = (
                (self.half, (0,)),
                *((flip, (0,)) for flip in inner),
                *((flip, (self.half,)) for flip in inner),
            )
            self.turns = tuple((i + self.half, i) for i in reversed(range(self.half)))
        self.held = (0, *(flip ^ block for flip, blocks in self.routes for block in blocks))
        self.landed = tuple(reversed(range(self.half)))

    def back(self, step):
        pairs = []
        for s in range(self.count):
            taker = s // self.half
            for core, flip in zip((taker, 1 - taker), self.turns[step]):
                pairs.append((2 * s + core, 2 * (s ^ flip) + taker))
        return pairs


def gather(plan, own):
    rows = own.shape[0]
    blocks, received = {0: own}, []
    for flip, names in plan.routes:
        sent = [blocks[name] for name in names]
        sent = sent[0] if len(sent) == 1 else jnp.concatenate(sent, axis=0)
        received.append(lax.ppermute(sent, "seq", [(i, i ^ flip) for i in range(plan.count)]))
        for at, name in enumerate(names):
            blocks[flip ^ name] = received[-1][at * rows : (at + 1) * rows]
    return received


def direct(plan, queries, latent, key_basis, value_basis, out_weight):
    rows = queries.shape[0]
    weights = key_basis, value_basis, out_weight
    own = jnp.concatenate([queries, latent.T], axis=1)
    own = pack(own, sum(2 * w.size for w in weights))
    received = gather(plan, own)
    keep, send = mix(plan, own, received, *weights)
    other = lax.ppermute(send, "head", [(0, 1), (1, 0)])
    total = (keep + other).astype(jnp.bfloat16)
    parts = [
        lax.ppermute(total[step * rows : (step + 1) * rows], ("seq", "head"), plan.back(step))
        for step in plan.landed
    ]
    return place(plan, parts)


def attend(queries, latent, key_basis, value_basis):
    tok_rows = queries.shape[0]
    head_count = key_basis.shape[1] // HEAD_DIM
    rank_count = key_basis.shape[0]
    score_scale = 1.0 / math.sqrt(HEAD_DIM)
    query_heads = queries.reshape(tok_rows, head_count, HEAD_DIM).transpose(1, 0, 2)
    key_maps = key_basis.reshape(rank_count, head_count, HEAD_DIM).transpose(1, 0, 2)
    value_maps = value_basis.reshape(rank_count, head_count, HEAD_DIM).transpose(1, 0, 2)

    def one_head(operands):
        query_one, key_map, value_map = operands
        key_rows = lax.dot_general(
            latent, key_map, (((0,), (0,)), ((), ())), preferred_element_type=jnp.float32
        ).astype(jnp.bfloat16)
        value_rows = lax.dot_general(
            latent, value_map, (((0,), (0,)), ((), ())), preferred_element_type=jnp.float32
        ).astype(jnp.bfloat16)
        scores = (
            lax.dot_general(query_one, key_rows, NT, preferred_element_type=jnp.float32)
            * score_scale
        )
        row_max = jnp.max(scores, axis=1, keepdims=True)
        weights = jnp.exp(scores - row_max)
        row_total = jnp.sum(weights, axis=1, keepdims=True)
        head_mixed = (
            jnp.dot(weights.astype(jnp.bfloat16), value_rows, preferred_element_type=jnp.float32)
            / row_total
        )
        return head_mixed.astype(jnp.bfloat16)

    mixed = lax.map(one_head, (query_heads, key_maps, value_maps))
    return mixed.transpose(1, 0, 2).reshape(tok_rows, head_count * HEAD_DIM)


def gathered(queries, latent, key_basis, value_basis, out_weight):
    latent = lax.all_gather(latent, "seq", axis=1, tiled=True)
    mixed = attend(queries, latent, key_basis, value_basis)
    weight = lax.all_gather(out_weight, "seq", axis=0, tiled=True)
    partial_value = lax.dot_general(mixed, weight, NT, preferred_element_type=jnp.float32)
    return lax.psum_scatter(partial_value, "head", scatter_dimension=1, tiled=True).astype(
        jnp.bfloat16
    )


def solution(mesh):
    placed = (
        P(("groups", "seq"), "head"),
        P(None, ("groups", "seq")),
        P(None, "head"),
        P(None, "head"),
        P("seq", "head"),
    )
    count = mesh.shape["seq"]
    pairwise = 4 <= count <= MOST_DIRECT and count & (count - 1) == 0 and mesh.shape["head"] == 2
    shards = functools.partial(direct, Plan(count)) if pairwise else gathered
    return jax.shard_map(
        shards, mesh=mesh, in_specs=placed, out_specs=P(("groups", "seq"), "head"), check_vma=False
    )
```

```python
import functools
import math

import jax
import jax.numpy as jnp
from jax import lax
from jax.experimental import pallas as pl
from jax.experimental.pallas import tpu as pltpu
from jax.sharding import PartitionSpec as P

HEAD_DIM = 128
MOST_DIRECT = 16
NT = (((1,), (1,)), ((), ()))


def turn_kernel(weight, turned):
    turned[...] = weight[...].T


def turn(weight):
    vmem = pl.BlockSpec(memory_space=pltpu.VMEM)
    return pl.pallas_call(
        turn_kernel,
        out_shape=jax.ShapeDtypeStruct(weight.shape[::-1], weight.dtype),
        in_specs=[vmem],
        out_specs=vmem,
        cost_estimate=pl.CostEstimate(
            flops=0, bytes_accessed=4 * weight.size, transcendentals=0
        ),
        compiler_params=pltpu.CompilerParams(vmem_limit_bytes=8 * 1024 * 1024),
        name="turn",
    )(weight)


def mix_kernel(plan, own, *refs):
    received = refs[: len(plan.routes)][::-1]
    key_basis, value_basis, out_weight, keep, send, partial_sum = refs[len(plan.routes) :]
    rows = own.shape[0]
    width = key_basis.shape[1]
    queries = jnp.concatenate([b[:, :width] for b in (own, *received)], axis=0)
    latent = jnp.concatenate([b[:, width:] for b in (own, *received)], axis=0)
    scale = 1.0 / math.sqrt(HEAD_DIM)
    heads = [slice(first, first + HEAD_DIM) for first in range(0, width, HEAD_DIM)]
    keys = jnp.dot(latent, key_basis[...], preferred_element_type=jnp.float32).astype(jnp.bfloat16)
    values = jnp.dot(latent, value_basis[...], preferred_element_type=jnp.float32).astype(
        jnp.bfloat16
    )
    scores = [
        lax.dot_general(queries[:, c], keys[:, c], NT, preferred_element_type=jnp.float32) * scale
        for c in heads
    ]
    weights = [jnp.exp(s - jnp.max(s, axis=1, keepdims=True)) for s in scores]
    totals = [jnp.sum(w, axis=1, keepdims=True) for w in weights]
    sums = [
        jnp.dot(w.astype(jnp.bfloat16), values[:, c], preferred_element_type=jnp.float32)
        for w, c in zip(weights, heads)
    ]
    mixed = jnp.concatenate([(s / t).astype(jnp.bfloat16) for s, t in zip(sums, totals)], axis=1)
    partial_sum[...] = jnp.dot(mixed, out_weight[...], preferred_element_type=jnp.float32)
    taker = lax.axis_index("head") == lax.axis_index("seq") // plan.half
    for step, flips in enumerate(plan.turns):
        first, second = (
            partial_sum[at * rows : (at + 1) * rows, :] for at in map(plan.held.index, flips)
        )
        part = slice(step * rows, (step + 1) * rows)
        keep[part, :] = jnp.where(taker, first, second)
        send[part, :] = jnp.where(taker, second, first)


def mix(plan, own, received, key_basis, value_basis, out_weight):
    rows = own.shape[0] * plan.count
    rank, width = key_basis.shape
    features = out_weight.shape[1]
    vmem = pl.BlockSpec(memory_space=pltpu.VMEM)
    return pl.pallas_call(
        functools.partial(mix_kernel, plan),
        out_shape=[jax.ShapeDtypeStruct((rows // 2, features), jnp.float32)] * 2,
        in_specs=[vmem] * (len(received) + 4),
        out_specs=[vmem] * 2,
        scratch_shapes=[pltpu.VMEM((rows, features), jnp.float32)],
        cost_estimate=pl.CostEstimate(
            flops=2 * rows * width * (2 * rank + 2 * rows + features),
            bytes_accessed=2 * width * (2 * rank + features),
            transcendentals=rows * rows * (width // HEAD_DIM),
        ),
        compiler_params=pltpu.CompilerParams(vmem_limit_bytes=16 * 1024 * 1024),
        name="mix",
    )(own, *received[::-1], key_basis, value_basis, out_weight)


def place_kernel(plan, *refs):
    parts, out = refs[:-1], refs[-1]
    features = parts[0].shape[1]
    seq = lax.axis_index("seq")
    near = seq // plan.half == lax.axis_index("head")
    for step, part in zip(plan.landed, parts):
        low, high = sorted(plan.turns[step])
        flip = jnp.where(near, low, high - plan.half)
        column = jnp.bitwise_xor(lax.rem(seq, plan.half), flip) * features
        out[:, pl.ds(pl.multiple_of(column, features), features)] = part[...]


def place(plan, parts):
    rows, features = parts[0].shape
    vmem = pl.BlockSpec(memory_space=pltpu.VMEM)
    return pl.pallas_call(
        functools.partial(place_kernel, plan),
        out_shape=jax.ShapeDtypeStruct((rows, features * plan.half), parts[0].dtype),
        in_specs=[vmem] * len(parts),
        out_specs=vmem,
        compiler_params=pltpu.CompilerParams(vmem_limit_bytes=1024 * 1024),
        name="place",
    )(*parts)


def pack_kernel(block, own):
    own[...] = block[...]


def pack(block, meanwhile):
    vmem = pl.BlockSpec(memory_space=pltpu.VMEM)
    return pl.pallas_call(
        pack_kernel,
        out_shape=jax.ShapeDtypeStruct(block.shape, block.dtype),
        in_specs=[vmem],
        out_specs=vmem,
        cost_estimate=pl.CostEstimate(
            flops=4096 * meanwhile, bytes_accessed=0, transcendentals=0
        ),
        compiler_params=pltpu.CompilerParams(vmem_limit_bytes=1024 * 1024),
        name="pack",
    )(block)


class Plan:
    def __init__(self, count):
        self.count, self.half = count, count // 2
        if count == 8:
            self.routes = ((1, (0,)), (6, (0,)), (4, (0,)), (2, (0,)), (4, (1,)), (2, (1,)), (1, (6,)))
            self.turns = ((5, 3), (6, 0), (7, 2), (4, 1))
        else:
            inner = tuple(reversed(range(1, self.half)))
            self.routes = (
                (self.half, (0,)),
                *((flip, (0,)) for flip in inner),
                *((flip, (self.half,)) for flip in inner),
            )
            self.turns = tuple((i + self.half, i) for i in reversed(range(self.half)))
        self.held = (0, *(flip ^ block for flip, blocks in self.routes for block in blocks))
        self.landed = tuple(reversed(range(self.half)))

    def back(self, step):
        pairs = []
        for s in range(self.count):
            taker = s // self.half
            for core, flip in zip((taker, 1 - taker), self.turns[step]):
                pairs.append((2 * s + core, 2 * (s ^ flip) + taker))
        return pairs


def gather(plan, own):
    rows = own.shape[0]
    blocks, received = {0: own}, []
    for flip, names in plan.routes:
        sent = [blocks[name] for name in names]
        sent = sent[0] if len(sent) == 1 else jnp.concatenate(sent, axis=0)
        received.append(lax.ppermute(sent, "seq", [(i, i ^ flip) for i in range(plan.count)]))
        for at, name in enumerate(names):
            blocks[flip ^ name] = received[-1][at * rows : (at + 1) * rows]
    return received


def direct(plan, queries, latent, key_basis, value_basis, out_weight):
    rows = queries.shape[0]
    weights = key_basis, value_basis, out_weight
    own = jnp.concatenate([queries, latent.T], axis=1)
    own = pack(own, sum(2 * w.size for w in weights))
    received = gather(plan, own)
    keep, send = mix(plan, own, received, key_basis, value_basis, turn(out_weight))
    other = lax.ppermute(send, "head", [(0, 1), (1, 0)])
    total = (keep + other).astype(jnp.bfloat16)
    parts = [
        lax.ppermute(total[step * rows : (step + 1) * rows], ("seq", "head"), plan.back(step))
        for step in plan.landed
    ]
    return place(plan, parts)


def attend(queries, latent, key_basis, value_basis):
    tok_rows = queries.shape[0]
    head_count = key_basis.shape[1] // HEAD_DIM
    rank_count = key_basis.shape[0]
    score_scale = 1.0 / math.sqrt(HEAD_DIM)
    query_heads = queries.reshape(tok_rows, head_count, HEAD_DIM).transpose(1, 0, 2)
    key_maps = key_basis.reshape(rank_count, head_count, HEAD_DIM).transpose(1, 0, 2)
    value_maps = value_basis.reshape(rank_count, head_count, HEAD_DIM).transpose(1, 0, 2)

    def one_head(operands):
        query_one, key_map, value_map = operands
        key_rows = lax.dot_general(
            latent, key_map, (((0,), (0,)), ((), ())), preferred_element_type=jnp.float32
        ).astype(jnp.bfloat16)
        value_rows = lax.dot_general(
            latent, value_map, (((0,), (0,)), ((), ())), preferred_element_type=jnp.float32
        ).astype(jnp.bfloat16)
        scores = (
            lax.dot_general(query_one, key_rows, NT, preferred_element_type=jnp.float32)
            * score_scale
        )
        row_max = jnp.max(scores, axis=1, keepdims=True)
        weights = jnp.exp(scores - row_max)
        row_total = jnp.sum(weights, axis=1, keepdims=True)
        head_mixed = (
            jnp.dot(weights.astype(jnp.bfloat16), value_rows, preferred_element_type=jnp.float32)
            / row_total
        )
        return head_mixed.astype(jnp.bfloat16)

    mixed = lax.map(one_head, (query_heads, key_maps, value_maps))
    return mixed.transpose(1, 0, 2).reshape(tok_rows, head_count * HEAD_DIM)


def gathered(queries, latent, key_basis, value_basis, out_weight):
    latent = lax.all_gather(latent, "seq", axis=1, tiled=True)
    mixed = attend(queries, latent, key_basis, value_basis)
    weight = lax.all_gather(out_weight, "seq", axis=0, tiled=True)
    partial_value = lax.dot_general(mixed, weight, NT, preferred_element_type=jnp.float32)
    return lax.psum_scatter(partial_value, "head", scatter_dimension=1, tiled=True).astype(
        jnp.bfloat16
    )


def solution(mesh):
    placed = (
        P(("groups", "seq"), "head"),
        P(None, ("groups", "seq")),
        P(None, "head"),
        P(None, "head"),
        P("seq", "head"),
    )
    count = mesh.shape["seq"]
    pairwise = 4 <= count <= MOST_DIRECT and count & (count - 1) == 0 and mesh.shape["head"] == 2
    shards = functools.partial(direct, Plan(count)) if pairwise else gathered
    return jax.shard_map(
        shards, mesh=mesh, in_specs=placed, out_specs=P(("groups", "seq"), "head"), check_vma=False
    )
```

```python
import functools
import math

import jax
import jax.numpy as jnp
from jax import lax
from jax.experimental import pallas as pl
from jax.experimental.pallas import tpu as pltpu
from jax.sharding import PartitionSpec as P

HEAD_DIM = 128
MOST_DIRECT = 8
NT = (((1,), (1,)), ((), ()))


def turn_kernel(weight, turned):
    turned[...] = weight[...].T


def turn(weight):
    vmem = pl.BlockSpec(memory_space=pltpu.VMEM)
    return pl.pallas_call(
        turn_kernel,
        out_shape=jax.ShapeDtypeStruct(weight.shape[::-1], weight.dtype),
        in_specs=[vmem],
        out_specs=vmem,
        cost_estimate=pl.CostEstimate(
            flops=0, bytes_accessed=4 * weight.size, transcendentals=0
        ),
        compiler_params=pltpu.CompilerParams(vmem_limit_bytes=8 * 1024 * 1024),
        name="turn",
    )(weight)


def mix_kernel(plan, own, *refs):
    received = refs[: len(plan.routes)][::-1]
    key_basis, value_basis, out_weight, keep, send, partial_sum = refs[len(plan.routes) :]
    rows = own.shape[0]
    width = key_basis.shape[1]
    queries = jnp.concatenate([b[:, :width] for b in (own, *received)], axis=0)
    latent = jnp.concatenate([b[:, width:] for b in (own, *received)], axis=0)
    scale = 1.0 / math.sqrt(HEAD_DIM)
    heads = [slice(first, first + HEAD_DIM) for first in range(0, width, HEAD_DIM)]
    keys = jnp.dot(latent, key_basis[...], preferred_element_type=jnp.float32).astype(jnp.bfloat16)
    values = jnp.dot(latent, value_basis[...], preferred_element_type=jnp.float32).astype(
        jnp.bfloat16
    )
    scores = [
        lax.dot_general(queries[:, c], keys[:, c], NT, preferred_element_type=jnp.float32) * scale
        for c in heads
    ]
    weights = [jnp.exp(s - jnp.max(s, axis=1, keepdims=True)) for s in scores]
    totals = [jnp.sum(w, axis=1, keepdims=True) for w in weights]
    sums = [
        jnp.dot(w.astype(jnp.bfloat16), values[:, c], preferred_element_type=jnp.float32)
        for w, c in zip(weights, heads)
    ]
    mixed = jnp.concatenate([(s / t).astype(jnp.bfloat16) for s, t in zip(sums, totals)], axis=1)
    partial_sum[...] = jnp.dot(mixed, out_weight[...], preferred_element_type=jnp.float32)
    core = lax.axis_index("head")
    for step in range(plan.half):
        part = slice(step * rows, (step + 1) * rows)
        for target, other in ((keep, 0), (send, 1)):
            at = jnp.where(
                core == 0,
                look_up(plan.kept(0, step, other)),
                look_up(plan.kept(1, step, 1 - other)),
            )
            target[part, :] = partial_sum[pl.ds(pl.multiple_of(at * rows, rows), rows), :]


def mix(plan, own, received, key_basis, value_basis, out_weight):
    rows = own.shape[0] * plan.count
    rank, width = key_basis.shape
    features = out_weight.shape[1]
    vmem = pl.BlockSpec(memory_space=pltpu.VMEM)
    return pl.pallas_call(
        functools.partial(mix_kernel, plan),
        out_shape=[jax.ShapeDtypeStruct((rows // 2, features), jnp.float32)] * 2,
        in_specs=[vmem] * (len(received) + 4),
        out_specs=[vmem] * 2,
        scratch_shapes=[pltpu.VMEM((rows, features), jnp.float32)],
        cost_estimate=pl.CostEstimate(
            flops=2 * rows * width * (2 * rank + 2 * rows + features),
            bytes_accessed=2 * width * (2 * rank + features),
            transcendentals=rows * rows * (width // HEAD_DIM),
        ),
        compiler_params=pltpu.CompilerParams(vmem_limit_bytes=16 * 1024 * 1024),
        name="mix",
    )(own, *received[::-1], key_basis, value_basis, out_weight)


def place_kernel(plan, *refs):
    parts, out = refs[:-1], refs[-1]
    features = parts[0].shape[1]
    core = lax.axis_index("head")
    for step, part in zip(reversed(range(plan.half)), parts):
        column = features * jnp.where(
            core == 0, look_up(plan.source(step, 0)), look_up(plan.source(step, 1))
        )
        out[:, pl.ds(pl.multiple_of(column, features), features)] = part[...]


def place(plan, parts):
    rows, features = parts[0].shape
    vmem = pl.BlockSpec(memory_space=pltpu.VMEM)
    return pl.pallas_call(
        functools.partial(place_kernel, plan),
        out_shape=jax.ShapeDtypeStruct((rows, features * plan.half), parts[0].dtype),
        in_specs=[vmem] * len(parts),
        out_specs=vmem,
        compiler_params=pltpu.CompilerParams(vmem_limit_bytes=1024 * 1024),
        name="place",
    )(*parts)


def pack_kernel(block, own):
    own[...] = block[...]


def pack(block, meanwhile):
    vmem = pl.BlockSpec(memory_space=pltpu.VMEM)
    return pl.pallas_call(
        pack_kernel,
        out_shape=jax.ShapeDtypeStruct(block.shape, block.dtype),
        in_specs=[vmem],
        out_specs=vmem,
        cost_estimate=pl.CostEstimate(
            flops=4096 * meanwhile, bytes_accessed=0, transcendentals=0
        ),
        compiler_params=pltpu.CompilerParams(vmem_limit_bytes=1024 * 1024),
        name="pack",
    )(block)


class Plan:
    def __init__(self, count):
        self.count, self.half = count, count // 2
        if count == 8:
            self.routes = (
                (0, 1, 1),
                (0, 6, 6),
                (0, 4, 4),
                (0, 2, 2),
                (1, 4, 4),
                (1, 2, 2),
                (2, 1, 1),
            )
            self.ways = (
                ((3, 7, 6, 1), (5, 4, 2, 0)),
                ((0, 6, 5, 3), (1, 2, 4, 7)),
                ((4, 3, 7, 5), (6, 1, 0, 2)),
                ((2, 5, 1, 4), (7, 0, 3, 6)),
                ((5, 4, 3, 7), (1, 2, 6, 0)),
                ((7, 6, 4, 5), (2, 3, 0, 1)),
                ((6, 1, 5, 3), (4, 0, 7, 2)),
                ((3, 7, 1, 6), (0, 5, 2, 4)),
            )
        else:
            inner = range(1, self.half)
            self.routes = (
                (0, self.half, self.half),
                *((0, flip, flip) for flip in inner),
                *((1, flip, flip) for flip in inner),
            )
            steps = range(self.half)
            self.ways = tuple(
                tuple(
                    tuple(s ^ (step + self.half * (core == s // self.half)) for step in steps)
                    for core in (0, 1)
                )
                for s in range(count)
            )

    def out(self, flips):
        return [(2 * s + h, 2 * (s ^ flips[h]) + h) for s in range(self.count) for h in (0, 1)]

    def held(self, core):
        flips = [0]
        for block, *steps in self.routes:
            flips.append(flips[block] ^ steps[core])
        return flips

    def back(self, step):
        return [
            (2 * s + h, 2 * self.ways[s][h][step] + s // self.half)
            for s in range(self.count)
            for h in (0, 1)
        ]

    def kept(self, core, step, sender):
        held = self.held(core)
        return [held.index(s ^ self.ways[s][sender][step]) for s in range(self.count)]

    def source(self, step, taker):
        source = [0] * self.count
        for sender, target in self.back(step):
            if target % 2 == taker:
                source[target // 2] = sender // 2 % self.half
        return source


def look_up(values):
    packed = sum(value << (3 * at) for at, value in enumerate(values))
    return jnp.bitwise_and(lax.shift_right_logical(packed, 3 * lax.axis_index("seq")), 7)


def gather(plan, own):
    blocks = [own]
    for block, *flips in plan.routes:
        blocks.append(lax.ppermute(blocks[block], ("seq", "head"), plan.out(flips)))
    return blocks[1:]


def direct(plan, queries, latent, key_basis, value_basis, out_weight):
    rows = queries.shape[0]
    weights = key_basis, value_basis, out_weight
    own = jnp.concatenate([queries, latent.T], axis=1)
    own = pack(own, sum(2 * w.size for w in weights))
    received = gather(plan, own)
    keep, send = mix(plan, own, received, key_basis, value_basis, turn(out_weight))
    other = lax.ppermute(send, "head", [(0, 1), (1, 0)])
    total = (keep + other).astype(jnp.bfloat16)
    parts = [
        lax.ppermute(total[step * rows : (step + 1) * rows], ("seq", "head"), plan.back(step))
        for step in reversed(range(plan.half))
    ]
    return place(plan, parts)


def attend(queries, latent, key_basis, value_basis):
    tok_rows = queries.shape[0]
    head_count = key_basis.shape[1] // HEAD_DIM
    rank_count = key_basis.shape[0]
    score_scale = 1.0 / math.sqrt(HEAD_DIM)
    query_heads = queries.reshape(tok_rows, head_count, HEAD_DIM).transpose(1, 0, 2)
    key_maps = key_basis.reshape(rank_count, head_count, HEAD_DIM).transpose(1, 0, 2)
    value_maps = value_basis.reshape(rank_count, head_count, HEAD_DIM).transpose(1, 0, 2)

    def one_head(operands):
        query_one, key_map, value_map = operands
        key_rows = lax.dot_general(
            latent, key_map, (((0,), (0,)), ((), ())), preferred_element_type=jnp.float32
        ).astype(jnp.bfloat16)
        value_rows = lax.dot_general(
            latent, value_map, (((0,), (0,)), ((), ())), preferred_element_type=jnp.float32
        ).astype(jnp.bfloat16)
        scores = (
            lax.dot_general(query_one, key_rows, NT, preferred_element_type=jnp.float32)
            * score_scale
        )
        row_max = jnp.max(scores, axis=1, keepdims=True)
        weights = jnp.exp(scores - row_max)
        row_total = jnp.sum(weights, axis=1, keepdims=True)
        head_mixed = (
            jnp.dot(weights.astype(jnp.bfloat16), value_rows, preferred_element_type=jnp.float32)
            / row_total
        )
        return head_mixed.astype(jnp.bfloat16)

    mixed = lax.map(one_head, (query_heads, key_maps, value_maps))
    return mixed.transpose(1, 0, 2).reshape(tok_rows, head_count * HEAD_DIM)


def gathered(queries, latent, key_basis, value_basis, out_weight):
    latent = lax.all_gather(latent, "seq", axis=1, tiled=True)
    mixed = attend(queries, latent, key_basis, value_basis)
    weight = lax.all_gather(out_weight, "seq", axis=0, tiled=True)
    partial_value = lax.dot_general(mixed, weight, NT, preferred_element_type=jnp.float32)
    return lax.psum_scatter(partial_value, "head", scatter_dimension=1, tiled=True).astype(
        jnp.bfloat16
    )


def solution(mesh):
    placed = (
        P(("groups", "seq"), "head"),
        P(None, ("groups", "seq")),
        P(None, "head"),
        P(None, "head"),
        P("seq", "head"),
    )
    count = mesh.shape["seq"]
    pairwise = 4 <= count <= MOST_DIRECT and count & (count - 1) == 0 and mesh.shape["head"] == 2
    shards = functools.partial(direct, Plan(count)) if pairwise else gathered
    return jax.shard_map(
        shards, mesh=mesh, in_specs=placed, out_specs=P(("groups", "seq"), "head"), check_vma=False
    )
```

```python
import functools
import math

import jax
import jax.numpy as jnp
from jax import lax
from jax.experimental import pallas as pl
from jax.experimental.pallas import tpu as pltpu
from jax.sharding import PartitionSpec as P

HEAD_DIM = 128
MOST_DIRECT = 8
NT = (((1,), (1,)), ((), ()))


def turn_kernel(weight, turned):
    turned[...] = weight[...].T


def turn(weight):
    vmem = pl.BlockSpec(memory_space=pltpu.VMEM)
    return pl.pallas_call(
        turn_kernel,
        out_shape=jax.ShapeDtypeStruct(weight.shape[::-1], weight.dtype),
        in_specs=[vmem],
        out_specs=vmem,
        cost_estimate=pl.CostEstimate(
            flops=0, bytes_accessed=4 * weight.size, transcendentals=0
        ),
        compiler_params=pltpu.CompilerParams(vmem_limit_bytes=8 * 1024 * 1024),
        name="turn",
    )(weight)


def mix_kernel(plan, own, *refs):
    received = refs[: len(plan.routes)][::-1]
    key_basis, value_basis, out_weight, keep, send, partial_sum = refs[len(plan.routes) :]
    rows = own.shape[0]
    width = key_basis.shape[1]
    queries = jnp.concatenate([b[:, :width] for b in (own, *received)], axis=0)
    latent = jnp.concatenate([b[:, width:] for b in (own, *received)], axis=0)
    scale = 1.0 / math.sqrt(HEAD_DIM)
    heads = [slice(first, first + HEAD_DIM) for first in range(0, width, HEAD_DIM)]
    values = jnp.dot(latent, value_basis[...], preferred_element_type=jnp.float32).astype(
        jnp.bfloat16
    )
    keys = jnp.dot(latent, key_basis[...], preferred_element_type=jnp.float32).astype(jnp.bfloat16)
    scores = [
        lax.dot_general(queries[:, c], keys[:, c], NT, preferred_element_type=jnp.float32) * scale
        for c in heads
    ]
    weights = [jnp.exp(s - jnp.max(s, axis=1, keepdims=True)) for s in scores]
    totals = [jnp.sum(w, axis=1, keepdims=True) for w in weights]
    sums = [
        jnp.dot(w.astype(jnp.bfloat16), values[:, c], preferred_element_type=jnp.float32)
        for w, c in zip(weights, heads)
    ]
    mixed = jnp.concatenate([(s / t).astype(jnp.bfloat16) for s, t in zip(sums, totals)], axis=1)
    partial_sum[...] = jnp.dot(mixed, out_weight[...], preferred_element_type=jnp.float32)
    core = lax.axis_index("head")
    for step in range(plan.half):
        part = slice(step * rows, (step + 1) * rows)
        for target, other in ((keep, 0), (send, 1)):
            at = jnp.where(
                core == 0,
                look_up(plan.kept(0, step, other)),
                look_up(plan.kept(1, step, 1 - other)),
            )
            target[part, :] = partial_sum[pl.ds(pl.multiple_of(at * rows, rows), rows), :]


def mix(plan, own, received, key_basis, value_basis, out_weight):
    rows = own.shape[0] * plan.count
    rank, width = key_basis.shape
    features = out_weight.shape[1]
    vmem = pl.BlockSpec(memory_space=pltpu.VMEM)
    return pl.pallas_call(
        functools.partial(mix_kernel, plan),
        out_shape=[jax.ShapeDtypeStruct((rows // 2, features), jnp.float32)] * 2,
        in_specs=[vmem] * (len(received) + 4),
        out_specs=[vmem] * 2,
        scratch_shapes=[pltpu.VMEM((rows, features), jnp.float32)],
        cost_estimate=pl.CostEstimate(
            flops=2 * rows * width * (2 * rank + 2 * rows + features),
            bytes_accessed=2 * width * (2 * rank + features),
            transcendentals=rows * rows * (width // HEAD_DIM),
        ),
        compiler_params=pltpu.CompilerParams(vmem_limit_bytes=16 * 1024 * 1024),
        name="mix",
    )(own, *received[::-1], key_basis, value_basis, out_weight)


def place_kernel(plan, *refs):
    parts, out = refs[:-1], refs[-1]
    features = parts[0].shape[1]
    core = lax.axis_index("head")
    for step, part in zip(reversed(range(plan.half)), parts):
        column = features * jnp.where(
            core == 0, look_up(plan.source(step, 0)), look_up(plan.source(step, 1))
        )
        out[:, pl.ds(pl.multiple_of(column, features), features)] = part[...]


def place(plan, parts):
    rows, features = parts[0].shape
    vmem = pl.BlockSpec(memory_space=pltpu.VMEM)
    return pl.pallas_call(
        functools.partial(place_kernel, plan),
        out_shape=jax.ShapeDtypeStruct((rows, features * plan.half), parts[0].dtype),
        in_specs=[vmem] * len(parts),
        out_specs=vmem,
        compiler_params=pltpu.CompilerParams(vmem_limit_bytes=1024 * 1024),
        name="place",
    )(*parts)


def pack_kernel(block, own):
    own[...] = block[...]


def pack(block, meanwhile):
    vmem = pl.BlockSpec(memory_space=pltpu.VMEM)
    return pl.pallas_call(
        pack_kernel,
        out_shape=jax.ShapeDtypeStruct(block.shape, block.dtype),
        in_specs=[vmem],
        out_specs=vmem,
        cost_estimate=pl.CostEstimate(
            flops=4096 * meanwhile, bytes_accessed=0, transcendentals=0
        ),
        compiler_params=pltpu.CompilerParams(vmem_limit_bytes=1024 * 1024),
        name="pack",
    )(block)


class Plan:
    def __init__(self, count):
        self.count, self.half = count, count // 2
        if count == 8:
            self.routes = (
                (0, 2, 1),
                (0, 1, 4),
                (0, 6, 2),
                (0, 4, 7),
                (2, 2, 2),
                (2, 4, 1),
                (3, 1, 1),
            )
            self.ways = (
                ((2, 6, 7, 1), (3, 5, 4, 0)),
                ((4, 2, 3, 7), (5, 0, 1, 6)),
                ((6, 1, 5, 3), (7, 4, 0, 2)),
                ((0, 7, 6, 5), (1, 3, 2, 4)),
                ((7, 4, 5, 6), (2, 1, 3, 0)),
                ((5, 7, 4, 3), (6, 2, 0, 1)),
                ((4, 0, 6, 5), (1, 3, 7, 2)),
                ((3, 5, 1, 7), (0, 6, 2, 4)),
            )
        else:
            inner = range(1, self.half)
            self.routes = (
                (0, self.half, self.half),
                *((0, flip, flip) for flip in inner),
                *((1, flip, flip) for flip in inner),
            )
            steps = range(self.half)
            self.ways = tuple(
                tuple(
                    tuple(s ^ (step + self.half * (core == s // self.half)) for step in steps)
                    for core in (0, 1)
                )
                for s in range(count)
            )

    def out(self, flips):
        return [(2 * s + h, 2 * (s ^ flips[h]) + h) for s in range(self.count) for h in (0, 1)]

    def held(self, core):
        flips = [0]
        for block, *steps in self.routes:
            flips.append(flips[block] ^ steps[core])
        return flips

    def back(self, step):
        return [
            (2 * s + h, 2 * self.ways[s][h][step] + s // self.half)
            for s in range(self.count)
            for h in (0, 1)
        ]

    def kept(self, core, step, sender):
        held = self.held(core)
        return [held.index(s ^ self.ways[s][sender][step]) for s in range(self.count)]

    def source(self, step, taker):
        source = [0] * self.count
        for sender, target in self.back(step):
            if target % 2 == taker:
                source[target // 2] = sender // 2 % self.half
        return source


def look_up(values):
    packed = sum(value << (3 * at) for at, value in enumerate(values))
    return jnp.bitwise_and(lax.shift_right_logical(packed, 3 * lax.axis_index("seq")), 7)


def gather(plan, own):
    blocks = [own]
    for block, *flips in plan.routes:
        blocks.append(lax.ppermute(blocks[block], ("seq", "head"), plan.out(flips)))
    return blocks[1:]


def direct(plan, queries, latent, key_basis, value_basis, out_weight):
    rows = queries.shape[0]
    weights = key_basis, value_basis, out_weight
    own = jnp.concatenate([queries, latent.T], axis=1)
    own = pack(own, sum(2 * w.size for w in weights))
    received = gather(plan, own)
    keep, send = mix(plan, own, received, key_basis, value_basis, turn(out_weight))
    other = lax.ppermute(send, "head", [(0, 1), (1, 0)])
    total = (keep + other).astype(jnp.bfloat16)
    parts = [
        lax.ppermute(total[step * rows : (step + 1) * rows], ("seq", "head"), plan.back(step))
        for step in reversed(range(plan.half))
    ]
    return place(plan, parts)


def attend(queries, latent, key_basis, value_basis):
    tok_rows = queries.shape[0]
    head_count = key_basis.shape[1] // HEAD_DIM
    rank_count = key_basis.shape[0]
    score_scale = 1.0 / math.sqrt(HEAD_DIM)
    query_heads = queries.reshape(tok_rows, head_count, HEAD_DIM).transpose(1, 0, 2)
    key_maps = key_basis.reshape(rank_count, head_count, HEAD_DIM).transpose(1, 0, 2)
    value_maps = value_basis.reshape(rank_count, head_count, HEAD_DIM).transpose(1, 0, 2)

    def one_head(operands):
        query_one, key_map, value_map = operands
        key_rows = lax.dot_general(
            latent, key_map, (((0,), (0,)), ((), ())), preferred_element_type=jnp.float32
        ).astype(jnp.bfloat16)
        value_rows = lax.dot_general(
            latent, value_map, (((0,), (0,)), ((), ())), preferred_element_type=jnp.float32
        ).astype(jnp.bfloat16)
        scores = (
            lax.dot_general(query_one, key_rows, NT, preferred_element_type=jnp.float32)
            * score_scale
        )
        row_max = jnp.max(scores, axis=1, keepdims=True)
        weights = jnp.exp(scores - row_max)
        row_total = jnp.sum(weights, axis=1, keepdims=True)
        head_mixed = (
            jnp.dot(weights.astype(jnp.bfloat16), value_rows, preferred_element_type=jnp.float32)
            / row_total
        )
        return head_mixed.astype(jnp.bfloat16)

    mixed = lax.map(one_head, (query_heads, key_maps, value_maps))
    return mixed.transpose(1, 0, 2).reshape(tok_rows, head_count * HEAD_DIM)


def gathered(queries, latent, key_basis, value_basis, out_weight):
    latent = lax.all_gather(latent, "seq", axis=1, tiled=True)
    mixed = attend(queries, latent, key_basis, value_basis)
    weight = lax.all_gather(out_weight, "seq", axis=0, tiled=True)
    partial_value = lax.dot_general(mixed, weight, NT, preferred_element_type=jnp.float32)
    return lax.psum_scatter(partial_value, "head", scatter_dimension=1, tiled=True).astype(
        jnp.bfloat16
    )


def solution(mesh):
    placed = (
        P(("groups", "seq"), "head"),
        P(None, ("groups", "seq")),
        P(None, "head"),
        P(None, "head"),
        P("seq", "head"),
    )
    count = mesh.shape["seq"]
    pairwise = 4 <= count <= MOST_DIRECT and count & (count - 1) == 0 and mesh.shape["head"] == 2
    shards = functools.partial(direct, Plan(count)) if pairwise else gathered
    return jax.shard_map(
        shards, mesh=mesh, in_specs=placed, out_specs=P(("groups", "seq"), "head"), check_vma=False
    )
```

```python
import functools
import math

import jax
import jax.numpy as jnp
from jax import lax
from jax.experimental import pallas as pl
from jax.experimental.pallas import tpu as pltpu
from jax.sharding import PartitionSpec as P

HEAD_DIM = 128
MOST_DIRECT = 8
NT = (((1,), (1,)), ((), ()))


def turn_kernel(weight, turned):
    turned[...] = weight[...].T


def turn(weight):
    vmem = pl.BlockSpec(memory_space=pltpu.VMEM)
    return pl.pallas_call(
        turn_kernel,
        out_shape=jax.ShapeDtypeStruct(weight.shape[::-1], weight.dtype),
        in_specs=[vmem],
        out_specs=vmem,
        cost_estimate=pl.CostEstimate(
            flops=0, bytes_accessed=4 * weight.size, transcendentals=0
        ),
        compiler_params=pltpu.CompilerParams(vmem_limit_bytes=8 * 1024 * 1024),
        name="turn",
    )(weight)


def mix_kernel(plan, own, *refs):
    received = refs[: len(plan.routes)][::-1]
    key_basis, value_basis, out_weight, keep, send, partial_sum = refs[len(plan.routes) :]
    rows = own.shape[0]
    width = key_basis.shape[1]
    queries = jnp.concatenate([b[:, :width] for b in (own, *received)], axis=0)
    latent = jnp.concatenate([b[:, width:] for b in (own, *received)], axis=0)
    scale = 1.0 / math.sqrt(HEAD_DIM)
    heads = [slice(first, first + HEAD_DIM) for first in range(0, width, HEAD_DIM)]
    keys = jnp.dot(latent, key_basis[...], preferred_element_type=jnp.float32).astype(jnp.bfloat16)
    values = jnp.dot(latent, value_basis[...], preferred_element_type=jnp.float32).astype(
        jnp.bfloat16
    )
    scores = [
        lax.dot_general(queries[:, c], keys[:, c], NT, preferred_element_type=jnp.float32) * scale
        for c in heads
    ]
    weights = [jnp.exp(s - jnp.max(s, axis=1, keepdims=True)) for s in scores]
    totals = [jnp.sum(w, axis=1, keepdims=True) for w in weights]
    sums = [
        jnp.dot(w.astype(jnp.bfloat16), values[:, c], preferred_element_type=jnp.float32)
        for w, c in zip(weights, heads)
    ]
    mixed = jnp.concatenate([(s / t).astype(jnp.bfloat16) for s, t in zip(sums, totals)], axis=1)
    partial_sum[...] = jnp.dot(mixed, out_weight[...], preferred_element_type=jnp.float32)
    core = lax.axis_index("head")
    for step in range(plan.half):
        part = slice(step * rows, (step + 1) * rows)
        for target, other in ((keep, 0), (send, 1)):
            at = jnp.where(
                core == 0,
                look_up(plan.kept(0, step, other)),
                look_up(plan.kept(1, step, 1 - other)),
            )
            target[part, :] = partial_sum[pl.ds(pl.multiple_of(at * rows, rows), rows), :].astype(
                target.dtype
            )


def mix(plan, own, received, key_basis, value_basis, out_weight):
    rows = own.shape[0] * plan.count
    rank, width = key_basis.shape
    features = out_weight.shape[1]
    vmem = pl.BlockSpec(memory_space=pltpu.VMEM)
    return pl.pallas_call(
        functools.partial(mix_kernel, plan),
        out_shape=[
            jax.ShapeDtypeStruct((rows // 2, features), kind)
            for kind in (jnp.float32, jnp.bfloat16)
        ],
        in_specs=[vmem] * (len(received) + 4),
        out_specs=[vmem] * 2,
        scratch_shapes=[pltpu.VMEM((rows, features), jnp.float32)],
        cost_estimate=pl.CostEstimate(
            flops=2 * rows * width * (2 * rank + 2 * rows + features),
            bytes_accessed=2 * width * (2 * rank + features),
            transcendentals=rows * rows * (width // HEAD_DIM),
        ),
        compiler_params=pltpu.CompilerParams(vmem_limit_bytes=16 * 1024 * 1024),
        name="mix",
    )(own, *received[::-1], key_basis, value_basis, out_weight)


def place_kernel(plan, *refs):
    parts, out = refs[:-1], refs[-1]
    features = parts[0].shape[1]
    core = lax.axis_index("head")
    for step, part in zip(reversed(range(plan.half)), parts):
        column = features * jnp.where(
            core == 0, look_up(plan.source(step, 0)), look_up(plan.source(step, 1))
        )
        out[:, pl.ds(pl.multiple_of(column, features), features)] = part[...]


def place(plan, parts):
    rows, features = parts[0].shape
    vmem = pl.BlockSpec(memory_space=pltpu.VMEM)
    return pl.pallas_call(
        functools.partial(place_kernel, plan),
        out_shape=jax.ShapeDtypeStruct((rows, features * plan.half), parts[0].dtype),
        in_specs=[vmem] * len(parts),
        out_specs=vmem,
        compiler_params=pltpu.CompilerParams(vmem_limit_bytes=1024 * 1024),
        name="place",
    )(*parts)


def pack_kernel(block, own):
    own[...] = block[...]


def pack(block, meanwhile):
    vmem = pl.BlockSpec(memory_space=pltpu.VMEM)
    return pl.pallas_call(
        pack_kernel,
        out_shape=jax.ShapeDtypeStruct(block.shape, block.dtype),
        in_specs=[vmem],
        out_specs=vmem,
        cost_estimate=pl.CostEstimate(
            flops=4096 * meanwhile, bytes_accessed=0, transcendentals=0
        ),
        compiler_params=pltpu.CompilerParams(vmem_limit_bytes=1024 * 1024),
        name="pack",
    )(block)


class Plan:
    def __init__(self, count):
        self.count, self.half = count, count // 2
        if count == 8:
            self.routes = (
                (0, 1, 1),
                (0, 6, 6),
                (0, 4, 4),
                (0, 2, 2),
                (1, 4, 4),
                (1, 2, 2),
                (2, 1, 1),
            )
            self.ways = (
                ((3, 7, 6, 1), (5, 4, 2, 0)),
                ((0, 6, 5, 3), (1, 2, 4, 7)),
                ((4, 3, 7, 5), (6, 1, 0, 2)),
                ((2, 5, 1, 4), (7, 0, 3, 6)),
                ((5, 4, 3, 7), (1, 2, 6, 0)),
                ((7, 6, 4, 5), (2, 3, 0, 1)),
                ((6, 1, 5, 3), (4, 0, 7, 2)),
                ((3, 7, 1, 6), (0, 5, 2, 4)),
            )
        else:
            inner = range(1, self.half)
            self.routes = (
                (0, self.half, self.half),
                *((0, flip, flip) for flip in inner),
                *((1, flip, flip) for flip in inner),
            )
            steps = range(self.half)
            self.ways = tuple(
                tuple(
                    tuple(s ^ (step + self.half * (core == s // self.half)) for step in steps)
                    for core in (0, 1)
                )
                for s in range(count)
            )

    def out(self, flips):
        return [(2 * s + h, 2 * (s ^ flips[h]) + h) for s in range(self.count) for h in (0, 1)]

    def held(self, core):
        flips = [0]
        for block, *steps in self.routes:
            flips.append(flips[block] ^ steps[core])
        return flips

    def back(self, step):
        return [
            (2 * s + h, 2 * self.ways[s][h][step] + s // self.half)
            for s in range(self.count)
            for h in (0, 1)
        ]

    def kept(self, core, step, sender):
        held = self.held(core)
        return [held.index(s ^ self.ways[s][sender][step]) for s in range(self.count)]

    def source(self, step, taker):
        source = [0] * self.count
        for sender, target in self.back(step):
            if target % 2 == taker:
                source[target // 2] = sender // 2 % self.half
        return source


def look_up(values):
    packed = sum(value << (3 * at) for at, value in enumerate(values))
    return jnp.bitwise_and(lax.shift_right_logical(packed, 3 * lax.axis_index("seq")), 7)


def gather(plan, own):
    blocks = [own]
    for block, *flips in plan.routes:
        blocks.append(lax.ppermute(blocks[block], ("seq", "head"), plan.out(flips)))
    return blocks[1:]


def direct(plan, queries, latent, key_basis, value_basis, out_weight):
    rows = queries.shape[0]
    weights = key_basis, value_basis, out_weight
    own = jnp.concatenate([queries, latent.T], axis=1)
    own = pack(own, sum(2 * w.size for w in weights))
    received = gather(plan, own)
    keep, send = mix(plan, own, received, key_basis, value_basis, turn(out_weight))
    other = lax.ppermute(send, "head", [(0, 1), (1, 0)])
    total = (keep + other).astype(jnp.bfloat16)
    parts = [
        lax.ppermute(total[step * rows : (step + 1) * rows], ("seq", "head"), plan.back(step))
        for step in reversed(range(plan.half))
    ]
    return place(plan, parts)


def attend(queries, latent, key_basis, value_basis):
    tok_rows = queries.shape[0]
    head_count = key_basis.shape[1] // HEAD_DIM
    rank_count = key_basis.shape[0]
    score_scale = 1.0 / math.sqrt(HEAD_DIM)
    query_heads = queries.reshape(tok_rows, head_count, HEAD_DIM).transpose(1, 0, 2)
    key_maps = key_basis.reshape(rank_count, head_count, HEAD_DIM).transpose(1, 0, 2)
    value_maps = value_basis.reshape(rank_count, head_count, HEAD_DIM).transpose(1, 0, 2)

    def one_head(operands):
        query_one, key_map, value_map = operands
        key_rows = lax.dot_general(
            latent, key_map, (((0,), (0,)), ((), ())), preferred_element_type=jnp.float32
        ).astype(jnp.bfloat16)
        value_rows = lax.dot_general(
            latent, value_map, (((0,), (0,)), ((), ())), preferred_element_type=jnp.float32
        ).astype(jnp.bfloat16)
        scores = (
            lax.dot_general(query_one, key_rows, NT, preferred_element_type=jnp.float32)
            * score_scale
        )
        row_max = jnp.max(scores, axis=1, keepdims=True)
        weights = jnp.exp(scores - row_max)
        row_total = jnp.sum(weights, axis=1, keepdims=True)
        head_mixed = (
            jnp.dot(weights.astype(jnp.bfloat16), value_rows, preferred_element_type=jnp.float32)
            / row_total
        )
        return head_mixed.astype(jnp.bfloat16)

    mixed = lax.map(one_head, (query_heads, key_maps, value_maps))
    return mixed.transpose(1, 0, 2).reshape(tok_rows, head_count * HEAD_DIM)


def gathered(queries, latent, key_basis, value_basis, out_weight):
    latent = lax.all_gather(latent, "seq", axis=1, tiled=True)
    mixed = attend(queries, latent, key_basis, value_basis)
    weight = lax.all_gather(out_weight, "seq", axis=0, tiled=True)
    partial_value = lax.dot_general(mixed, weight, NT, preferred_element_type=jnp.float32)
    return lax.psum_scatter(partial_value, "head", scatter_dimension=1, tiled=True).astype(
        jnp.bfloat16
    )


def solution(mesh):
    placed = (
        P(("groups", "seq"), "head"),
        P(None, ("groups", "seq")),
        P(None, "head"),
        P(None, "head"),
        P("seq", "head"),
    )
    count = mesh.shape["seq"]
    pairwise = 4 <= count <= MOST_DIRECT and count & (count - 1) == 0 and mesh.shape["head"] == 2
    shards = functools.partial(direct, Plan(count)) if pairwise else gathered
    return jax.shard_map(
        shards, mesh=mesh, in_specs=placed, out_specs=P(("groups", "seq"), "head"), check_vma=False
    )
```

```python
import functools
import math

import jax
import jax.numpy as jnp
from jax import lax
from jax.experimental import pallas as pl
from jax.experimental.pallas import tpu as pltpu
from jax.sharding import PartitionSpec as P

HEAD_DIM = 128
MOST_DIRECT = 8
NT = (((1,), (1,)), ((), ()))


def turn_kernel(weight, turned):
    turned[...] = weight[...].T


def turn(weight):
    vmem = pl.BlockSpec(memory_space=pltpu.VMEM)
    return pl.pallas_call(
        turn_kernel,
        out_shape=jax.ShapeDtypeStruct(weight.shape[::-1], weight.dtype),
        in_specs=[vmem],
        out_specs=vmem,
        cost_estimate=pl.CostEstimate(
            flops=0, bytes_accessed=4 * weight.size, transcendentals=0
        ),
        compiler_params=pltpu.CompilerParams(vmem_limit_bytes=8 * 1024 * 1024),
        name="turn",
    )(weight)


def mix_kernel(plan, own, *refs):
    received = refs[: len(plan.routes)][::-1]
    key_basis, value_basis, out_weight, keep, send, partial_sum = refs[len(plan.routes) :]
    rows = own.shape[0]
    width = key_basis.shape[1]
    queries = jnp.concatenate([b[:, :width] for b in (own, *received)], axis=0)
    latent = jnp.concatenate([b[:, width:] for b in (own, *received)], axis=0)
    scale = 1.0 / math.sqrt(HEAD_DIM)
    heads = [slice(first, first + HEAD_DIM) for first in range(0, width, HEAD_DIM)]
    keys = jnp.dot(latent, key_basis[...], preferred_element_type=jnp.float32).astype(jnp.bfloat16)
    values = jnp.dot(latent, value_basis[...], preferred_element_type=jnp.float32).astype(
        jnp.bfloat16
    )
    scores = [
        lax.dot_general(queries[:, c], keys[:, c], NT, preferred_element_type=jnp.float32) * scale
        for c in heads
    ]
    weights = [jnp.exp(s - jnp.max(s, axis=1, keepdims=True)) for s in scores]
    totals = [jnp.sum(w, axis=1, keepdims=True) for w in weights]
    sums = [
        jnp.dot(w.astype(jnp.bfloat16), values[:, c], preferred_element_type=jnp.float32)
        for w, c in zip(weights, heads)
    ]
    mixed = jnp.concatenate([(s / t).astype(jnp.bfloat16) for s, t in zip(sums, totals)], axis=1)
    partial_sum[...] = jnp.dot(mixed, out_weight[...], preferred_element_type=jnp.float32)
    core = lax.axis_index("head")
    for step in range(plan.half):
        part = slice(step * rows, (step + 1) * rows)
        for target, other in ((keep, 0), (send, 1)):
            at = jnp.where(
                core == 0,
                look_up(plan.kept(0, step, other)),
                look_up(plan.kept(1, step, 1 - other)),
            )
            target[part, :] = partial_sum[pl.ds(pl.multiple_of(at * rows, rows), rows), :]


def mix(plan, own, received, key_basis, value_basis, out_weight):
    rows = own.shape[0] * plan.count
    rank, width = key_basis.shape
    features = out_weight.shape[1]
    vmem = pl.BlockSpec(memory_space=pltpu.VMEM)
    return pl.pallas_call(
        functools.partial(mix_kernel, plan),
        out_shape=[jax.ShapeDtypeStruct((rows // 2, features), jnp.float32)] * 2,
        in_specs=[vmem] * (len(received) + 4),
        out_specs=[vmem] * 2,
        scratch_shapes=[pltpu.VMEM((rows, features), jnp.float32)],
        cost_estimate=pl.CostEstimate(
            flops=2 * rows * width * (2 * rank + 2 * rows + features),
            bytes_accessed=2 * width * (2 * rank + features),
            transcendentals=rows * rows * (width // HEAD_DIM),
        ),
        compiler_params=pltpu.CompilerParams(vmem_limit_bytes=16 * 1024 * 1024),
        name="mix",
    )(own, *received[::-1], key_basis, value_basis, out_weight)


def place_kernel(plan, *refs):
    parts, out = refs[:-1], refs[-1]
    features = parts[0].shape[1]
    core = lax.axis_index("head")
    for step, part in zip(reversed(range(plan.half)), parts):
        column = features * jnp.where(
            core == 0, look_up(plan.source(step, 0)), look_up(plan.source(step, 1))
        )
        out[:, pl.ds(pl.multiple_of(column, features), features)] = part[...]


def place(plan, parts):
    rows, features = parts[0].shape
    vmem = pl.BlockSpec(memory_space=pltpu.VMEM)
    return pl.pallas_call(
        functools.partial(place_kernel, plan),
        out_shape=jax.ShapeDtypeStruct((rows, features * plan.half), parts[0].dtype),
        in_specs=[vmem] * len(parts),
        out_specs=vmem,
        compiler_params=pltpu.CompilerParams(vmem_limit_bytes=1024 * 1024),
        name="place",
    )(*parts)


def pack_kernel(block, own):
    own[...] = block[...]


def pack(block, meanwhile):
    vmem = pl.BlockSpec(memory_space=pltpu.VMEM)
    return pl.pallas_call(
        pack_kernel,
        out_shape=jax.ShapeDtypeStruct(block.shape, block.dtype),
        in_specs=[vmem],
        out_specs=vmem,
        cost_estimate=pl.CostEstimate(
            flops=4096 * meanwhile, bytes_accessed=0, transcendentals=0
        ),
        compiler_params=pltpu.CompilerParams(vmem_limit_bytes=1024 * 1024),
        name="pack",
    )(block)


class Plan:
    def __init__(self, count):
        self.count, self.half = count, count // 2
        if count == 8:
            self.routes = (
                (0, 1, 1),
                (0, 6, 6),
                (0, 4, 4),
                (0, 2, 2),
                (1, 4, 4),
                (1, 2, 2),
                (2, 1, 1),
            )
            self.ways = (
                ((4, 7, 6, 2), (3, 5, 1, 0)),
                ((5, 4, 3, 7), (1, 0, 2, 6)),
                ((7, 1, 5, 3), (6, 2, 0, 4)),
                ((0, 6, 4, 5), (2, 3, 7, 1)),
                ((4, 1, 7, 5), (6, 2, 3, 0)),
                ((5, 7, 2, 3), (0, 6, 4, 1)),
                ((7, 4, 0, 6), (1, 3, 5, 2)),
                ((3, 5, 6, 7), (2, 0, 1, 4)),
            )
        else:
            inner = range(1, self.half)
            self.routes = (
                (0, self.half, self.half),
                *((0, flip, flip) for flip in inner),
                *((1, flip, flip) for flip in inner),
            )
            steps = range(self.half)
            self.ways = tuple(
                tuple(
                    tuple(s ^ (step + self.half * (core == s // self.half)) for step in steps)
                    for core in (0, 1)
                )
                for s in range(count)
            )

    def out(self, flips):
        return [(2 * s + h, 2 * (s ^ flips[h]) + h) for s in range(self.count) for h in (0, 1)]

    def held(self, core):
        flips = [0]
        for block, *steps in self.routes:
            flips.append(flips[block] ^ steps[core])
        return flips

    def back(self, step):
        return [
            (2 * s + h, 2 * self.ways[s][h][step] + s // self.half)
            for s in range(self.count)
            for h in (0, 1)
        ]

    def kept(self, core, step, sender):
        held = self.held(core)
        return [held.index(s ^ self.ways[s][sender][step]) for s in range(self.count)]

    def source(self, step, taker):
        source = [0] * self.count
        for sender, target in self.back(step):
            if target % 2 == taker:
                source[target // 2] = sender // 2 % self.half
        return source


def look_up(values):
    packed = sum(value << (3 * at) for at, value in enumerate(values))
    return jnp.bitwise_and(lax.shift_right_logical(packed, 3 * lax.axis_index("seq")), 7)


def gather(plan, own):
    blocks = [own]
    for block, *flips in plan.routes:
        blocks.append(lax.ppermute(blocks[block], ("seq", "head"), plan.out(flips)))
    return blocks[1:]


def direct(plan, queries, latent, key_basis, value_basis, out_weight):
    rows = queries.shape[0]
    weights = key_basis, value_basis, out_weight
    own = jnp.concatenate([queries, latent.T], axis=1)
    own = pack(own, sum(2 * w.size for w in weights))
    received = gather(plan, own)
    keep, send = mix(plan, own, received, key_basis, value_basis, turn(out_weight))
    other = lax.ppermute(send, "head", [(0, 1), (1, 0)])
    total = (keep + other).astype(jnp.bfloat16)
    parts = [
        lax.ppermute(total[step * rows : (step + 1) * rows], ("seq", "head"), plan.back(step))
        for step in reversed(range(plan.half))
    ]
    return place(plan, parts)


def attend(queries, latent, key_basis, value_basis):
    tok_rows = queries.shape[0]
    head_count = key_basis.shape[1] // HEAD_DIM
    rank_count = key_basis.shape[0]
    score_scale = 1.0 / math.sqrt(HEAD_DIM)
    query_heads = queries.reshape(tok_rows, head_count, HEAD_DIM).transpose(1, 0, 2)
    key_maps = key_basis.reshape(rank_count, head_count, HEAD_DIM).transpose(1, 0, 2)
    value_maps = value_basis.reshape(rank_count, head_count, HEAD_DIM).transpose(1, 0, 2)

    def one_head(operands):
        query_one, key_map, value_map = operands
        key_rows = lax.dot_general(
            latent, key_map, (((0,), (0,)), ((), ())), preferred_element_type=jnp.float32
        ).astype(jnp.bfloat16)
        value_rows = lax.dot_general(
            latent, value_map, (((0,), (0,)), ((), ())), preferred_element_type=jnp.float32
        ).astype(jnp.bfloat16)
        scores = (
            lax.dot_general(query_one, key_rows, NT, preferred_element_type=jnp.float32)
            * score_scale
        )
        row_max = jnp.max(scores, axis=1, keepdims=True)
        weights = jnp.exp(scores - row_max)
        row_total = jnp.sum(weights, axis=1, keepdims=True)
        head_mixed = (
            jnp.dot(weights.astype(jnp.bfloat16), value_rows, preferred_element_type=jnp.float32)
            / row_total
        )
        return head_mixed.astype(jnp.bfloat16)

    mixed = lax.map(one_head, (query_heads, key_maps, value_maps))
    return mixed.transpose(1, 0, 2).reshape(tok_rows, head_count * HEAD_DIM)


def gathered(queries, latent, key_basis, value_basis, out_weight):
    latent = lax.all_gather(latent, "seq", axis=1, tiled=True)
    mixed = attend(queries, latent, key_basis, value_basis)
    weight = lax.all_gather(out_weight, "seq", axis=0, tiled=True)
    partial_value = lax.dot_general(mixed, weight, NT, preferred_element_type=jnp.float32)
    return lax.psum_scatter(partial_value, "head", scatter_dimension=1, tiled=True).astype(
        jnp.bfloat16
    )


def solution(mesh):
    placed = (
        P(("groups", "seq"), "head"),
        P(None, ("groups", "seq")),
        P(None, "head"),
        P(None, "head"),
        P("seq", "head"),
    )
    count = mesh.shape["seq"]
    pairwise = 4 <= count <= MOST_DIRECT and count & (count - 1) == 0 and mesh.shape["head"] == 2
    shards = functools.partial(direct, Plan(count)) if pairwise else gathered
    return jax.shard_map(
        shards, mesh=mesh, in_specs=placed, out_specs=P(("groups", "seq"), "head"), check_vma=False
    )
```
